32 devices in a mesh: grp: 2 (over y), seq: 4 (over z), head: 4 (over x, core).
Axes of the slice: x: 2, y: 2, z: 4, core: 2. Of those that a mesh axis runs over, the one named last changes fastest.
Arguments:
- byte_ids: int32 [16384], P(('grp', 'seq')), parts along dimension 0, may hold values from 0 to 255, as said below
- queries: bfloat16 [4, 64, 16384], P('head', None, ('grp', 'seq')), parts along dimension 2, may hold values from -170 to 170
- key_states: bfloat16 [4, 64, 16384], P('head', None, ('grp', 'seq')), parts along dimension 2, may hold values from -12 to 12
- values: bfloat16 [4, 64, 16384], P('head', None, ('grp', 'seq')), parts along dimension 2, may hold values from -10 to 10
- cotangent: bfloat16 [4, 64, 16384], P('head', None, ('grp', 'seq')), parts along dimension 2, may hold values from -10 to 10
Outputs:
- attended: bfloat16 [4, 64, 16384], P('head', None, ('grp', 'seq')), parts along dimension 2
- grad_queries: bfloat16 [4, 64, 16384], P('head', None, ('grp', 'seq')), parts along dimension 2
- grad_keys: bfloat16 [4, 64, 16384], P('head', None, ('grp', 'seq')), parts along dimension 2
- grad_values: bfloat16 [4, 64, 16384], P('head', None, ('grp', 'seq')), parts along dimension 2
The draws below stay inside these ranges and needn't reach their ends.
There are 2 independent parts, one for each index of `grp`. The reference program is written for one: setup_inputs(seed, part) draws one part's arguments, and reference() takes and returns one part's arrays. A program takes and returns all parts, laid end to end along the dimension named above; each array names one. Nothing has to cross between parts.
Inputs may be any that keep to these rules, and one draw needn't show every extreme that they name: `byte_ids`: 0 marks a dropped byte, which is attended only by its own position.
All inputs are finite; a program needn't handle non-finite values.
Results may differ from the reference program's by a relative error of at most 0.0055.
Values sent between devices are 32-bit elements; how exact they have to be, the bound alone decides.
A program may use at most 64 MiB of HBM per device.

```python
import jax
import jax.numpy as jnp
from jax import lax

HEAD = 64
HEADS = 4
BLOCK = 128
TOK_DEV = 2048
TOKENS = 8192


def region_field(key, region, spread_value):
    table = jnp.clip(jax.random.normal(key, (HEADS, HEAD, TOKENS // 8), jnp.float32), -4.0, 4.0)
    positions = jnp.arange(TOKENS) // region
    return jnp.take(table, positions, axis=2) * spread_value


def shared_keys(key, rate, region):
    rough = jnp.clip(jax.random.normal(jax.random.fold_in(key, 101), (HEADS, HEAD, TOKENS), jnp.float32), -4.0, 4.0)
    offsets = region_field(jax.random.fold_in(key, 102), region, 1.0)
    even = (jnp.arange(TOKENS) % 2 == 0)[None, None, :]
    flags = jax.random.bernoulli(jax.random.fold_in(key, 103), rate, (HEADS, 1, TOKENS)) & even
    strength = jax.random.uniform(jax.random.fold_in(key, 104), (HEADS, 1, TOKENS), jnp.float32, 5.0, 15.0)
    spacing = jax.random.uniform(jax.random.fold_in(key, 105), (HEADS, 1, TOKENS), jnp.float32, 1.0, 3.0)
    return (1.8 * rough + offsets, flags, strength, spacing)


def draw_byte_ids(key, part):
    key = jax.random.fold_in(key, 5)
    dropped = jax.random.randint(jax.random.fold_in(key, 1), (TOKENS,), 0, 4) == 0
    chosen = jax.random.randint(jax.random.fold_in(key, 2), (TOKENS,), 1, 256)
    return jnp.where(dropped, 0, chosen).astype(jnp.int32)


def draw_queries(key, part):
    shared_k, flags, strength, spacing = shared_keys(key, 0.0, TOK_DEV // 2)
    region = TOK_DEV // 2
    key = jax.random.fold_in(key, 1)
    rough = jnp.clip(jax.random.normal(jax.random.fold_in(key, 11), (HEADS, HEAD, TOKENS), jnp.float32), -4.0, 4.0)
    own = 1.8 * rough + region_field(jax.random.fold_in(key, 12), region, 1.0)
    return jnp.where(flags, strength * shared_k, own).astype(jnp.bfloat16)


def draw_key_states(key, part):
    shared_k, flags, strength, spacing = shared_keys(key, 0.0, TOK_DEV // 2)
    before = jnp.roll(shared_k, 1, axis=2)
    flag_before = jnp.roll(flags, 1, axis=2)
    shrink = 1.0 - jnp.roll(spacing, 1, axis=2) / (34.0 * jnp.roll(strength, 1, axis=2))
    return jnp.where(flag_before, before * shrink, shared_k).astype(jnp.bfloat16)


def draw_values(key, part):
    key = jax.random.fold_in(key, 3)
    rough = jnp.clip(jax.random.normal(jax.random.fold_in(key, 21), (HEADS, HEAD, TOKENS), jnp.float32), -4.0, 4.0)
    region = TOK_DEV // 2
    return (rough + region_field(jax.random.fold_in(key, 22), region, 1.5)).astype(jnp.bfloat16)


def draw_cotangent(key, part):
    key = jax.random.fold_in(key, 4)
    rough = jnp.clip(jax.random.normal(jax.random.fold_in(key, 31), (HEADS, HEAD, TOKENS), jnp.float32), -4.0, 4.0)
    region = TOK_DEV // 2
    return (rough + region_field(jax.random.fold_in(key, 32), region, 1.5)).astype(jnp.bfloat16)


def setup_inputs(seed: int = 0, part: int = 0) -> dict:
    splits = jax.random.split(jax.random.key(seed), 6)
    part_splits = jax.random.split(jax.random.fold_in(splits[5], part), 6)
    byte_ids = draw_byte_ids(jax.random.fold_in(jax.random.fold_in(splits[5], part), 71), part)
    queries = draw_queries(jax.random.fold_in(jax.random.fold_in(splits[5], part), 71), part)
    key_states = draw_key_states(jax.random.fold_in(jax.random.fold_in(splits[5], part), 71), part)
    values = draw_values(jax.random.fold_in(jax.random.fold_in(splits[5], part), 71), part)
    cotangent = draw_cotangent(jax.random.fold_in(jax.random.fold_in(splits[5], part), 71), part)
    return dict(byte_ids=byte_ids, queries=queries, key_states=key_states, values=values, cotangent=cotangent)


far_below = -1.0e30
highest = lax.Precision.HIGHEST


def pair_sum(array):
    return array.reshape(array.shape[:-1] + (array.shape[-1] // 2, 2)).sum(-1)


def spread(array, times):
    return jnp.repeat(array, times, axis=-1)


def flat_rows(array):
    return array.reshape(array.shape[:-2] + (array.shape[-2] * array.shape[-1],))


def sibling(array, block):
    lead = array.shape[:-1]
    length = array.shape[-1]
    paired = array.reshape(lead + (length // (2 * block), 2, block))
    return jnp.flip(paired, axis=-2).reshape(lead + (length // block, block))


def unsibling(array):
    lead = array.shape[:-2]
    groups, block = array.shape[-2], array.shape[-1]
    paired = array.reshape(lead + (groups // 2, 2, block))
    return jnp.flip(paired, axis=-2).reshape(lead + (groups * block,))


def far_forward(query_mean, key_sib, value_sib, count_sib, score_scale):
    key_mean = key_sib / jnp.maximum(count_sib, 1.0)
    scores = jnp.einsum("hegr,hegb->hgrb", query_mean, key_mean, precision=highest) * score_scale
    live = (count_sib > 0)[:, None, :]
    masked = jnp.where(live, scores, far_below)
    far_top = masked.max(-1)
    weights = jnp.where(live, jnp.exp(masked - far_top[..., None]), 0.0)
    numer = jnp.einsum("hgrb,hegb->hegr", weights, value_sib, precision=highest)
    denom = jnp.einsum("hgrb,gb->hgr", weights, count_sib, precision=highest)
    return far_top, numer, denom, weights, key_mean


def far_backward(query_mean, key_mean, value_sib, count_sib, weights, row_grad, row_stat, score_scale):
    grad_value = jnp.einsum("hgrb,hegr->hegb", weights, row_grad, precision=highest)
    inner = jnp.einsum("hegr,hegb->hgrb", row_grad, value_sib, precision=highest)
    dscore = weights * (inner - count_sib[:, None, :] * row_stat[..., None])
    grad_query = score_scale * jnp.einsum("hgrb,hegb->hegr", dscore, key_mean, precision=highest)
    grad_key = score_scale * jnp.einsum("hgrb,hegr->hegb", dscore, query_mean, precision=highest)
    grad_key = grad_key / jnp.maximum(count_sib, 1.0)
    return grad_query, grad_key, grad_value


def head_pass(queries, key_states, values, cotangent, valid):
    score_scale = HEAD ** -0.5
    total = queries.shape[-1]
    top_level = (total // BLOCK).bit_length() - 2
    span = 2 * BLOCK
    pairs = total // span
    query_pairs = queries.astype(jnp.float32).reshape(1, HEAD, pairs, span)
    key_pairs = key_states.astype(jnp.float32).reshape(1, HEAD, pairs, span)
    value_pairs = values.astype(jnp.float32).reshape(1, HEAD, pairs, span)
    cot_full = cotangent.astype(jnp.float32).reshape(1, HEAD, total)
    cot_pairs = cot_full.reshape(1, HEAD, pairs, span)
    allowed = (valid.reshape(pairs, span)[:, None, :] > 0) | jnp.eye(span, dtype=bool)
    scores = jnp.einsum("hepi,hepj->hpij", query_pairs, key_pairs) * score_scale
    masked = jnp.where(allowed, scores, far_below)
    near_top = masked.max(-1)
    near_half = jnp.where(allowed, jnp.exp(masked - near_top[..., None]), 0.0).astype(jnp.bfloat16)
    near_half = lax.optimization_barrier(near_half)
    near_weight = near_half.astype(jnp.float32)
    near_num = jnp.einsum("hpij,hepj->hepi", near_weight, value_pairs).reshape(1, HEAD, total)
    near_den = near_weight.sum(-1).reshape(1, total)
    near_top = near_top.reshape(1, total)

    query_sum = queries.astype(jnp.float32)[None]
    key_sum = key_states.astype(jnp.float32)[None] * valid
    value_sum = values.astype(jnp.float32)[None] * valid
    counts = valid
    records = []
    for level in range(1, top_level + 1):
        query_sum = pair_sum(query_sum)
        key_sum = pair_sum(key_sum)
        value_sum = pair_sum(value_sum)
        counts = pair_sum(counts)
        groups = (total >> level) // BLOCK
        query_mean = (query_sum / 2.0 ** level).reshape(1, HEAD, groups, BLOCK)
        key_sib = sibling(key_sum, BLOCK)
        value_sib = sibling(value_sum, BLOCK)
        count_sib = sibling(counts, BLOCK)
        result = far_forward(query_mean, key_sib, value_sib, count_sib, score_scale)
        records.append((query_mean,) + result + (value_sib, count_sib))

    row_top = near_top
    for level in range(1, top_level + 1):
        row_top = jnp.maximum(row_top, spread(flat_rows(records[level - 1][1]), 2 ** level))
    near_factor = jnp.exp(near_top - row_top)
    numer = near_factor[:, None, :] * near_num
    denom = near_factor * near_den
    for level in range(1, top_level + 1):
        record = records[level - 1]
        factor = jnp.exp(spread(flat_rows(record[1]), 2 ** level) - row_top)
        numer = numer + factor[:, None, :] * spread(flat_rows(record[2]), 2 ** level)
        denom = denom + factor * spread(flat_rows(record[3]), 2 ** level)
    output = numer / denom[:, None, :]
    attended = output.astype(jnp.bfloat16)

    row_stat = jnp.sum(cot_full * output, axis=1)
    inverse = 1.0 / denom
    near_gain = near_factor * inverse
    scaled_half = (near_gain[:, None, :] * cot_full).astype(jnp.bfloat16)
    scaled_half = lax.optimization_barrier(scaled_half)
    scaled_cot = scaled_half.astype(jnp.float32).reshape(1, HEAD, pairs, span)
    near_dv = jnp.einsum("hpij,hepi->hepj", near_weight, scaled_cot)
    near_dprob = jnp.einsum("hepi,hepj->hpij", cot_pairs, value_pairs)
    gain_pairs = near_gain.reshape(1, pairs, span)
    stat_pairs = row_stat.reshape(1, pairs, span)
    dscore_half = (near_weight * gain_pairs[..., None] * (near_dprob - stat_pairs[..., None])).astype(jnp.bfloat16)
    dscore_half = lax.optimization_barrier(dscore_half)
    near_dscore = dscore_half.astype(jnp.float32)
    grad_q = score_scale * jnp.einsum("hpij,hepj->hepi", near_dscore, key_pairs).reshape(1, HEAD, total)
    grad_k = score_scale * jnp.einsum("hpij,hepi->hepj", near_dscore, query_pairs).reshape(1, HEAD, total)
    grad_v = near_dv.reshape(1, HEAD, total)

    for level in range(1, top_level + 1):
        record = records[level - 1]
        length = total >> level
        groups = length // BLOCK
        gain = jnp.exp(spread(flat_rows(record[1]), 2 ** level) - row_top) * inverse
        row_grad = (gain[:, None, :] * cot_full).reshape(1, HEAD, length, 2 ** level).sum(-1)
        row_grad = row_grad.reshape(1, HEAD, groups, BLOCK)
        level_stat = (gain * row_stat).reshape(1, length, 2 ** level).sum(-1).reshape(1, groups, BLOCK)
        grad_query, grad_key, grad_value = far_backward(record[0], record[5], record[6], record[7], record[4], row_grad, level_stat, score_scale)
        grad_q = grad_q + spread(flat_rows(grad_query) / 2.0 ** level, 2 ** level)
        grad_k = grad_k + valid * spread(unsibling(grad_key), 2 ** level)
        grad_v = grad_v + valid * spread(unsibling(grad_value), 2 ** level)
    return (attended[0], grad_q.astype(jnp.bfloat16)[0], grad_k.astype(jnp.bfloat16)[0], grad_v.astype(jnp.bfloat16)[0])


def reference(byte_ids, queries, key_states, values, cotangent):
    valid = (byte_ids != 0).astype(jnp.float32)

    def one_head(items):
        return head_pass(items[0], items[1], items[2], items[3], valid)

    results = lax.map(one_head, (queries, key_states, values, cotangent))
    return (results[0], results[1], results[2], results[3])
```

```python
import jax
import jax.numpy as jnp
from jax import lax
from jax.experimental import pallas as pl
from jax.experimental.pallas import tpu as pltpu
from jax.sharding import PartitionSpec as P

HEAD = 64
BLOCK = 128
SPAN = 256
NEAR_DEAD = -(2.0**96)
FAR_DEAD = -(2.0**90)
F32 = jnp.float32
BF16 = jnp.bfloat16


def nn(a, b):
    return lax.dot_general(a, b, (((1,), (0,)), ((), ())), preferred_element_type=F32)


def nt(a, b):
    return lax.dot_general(a, b, (((1,), (1,)), ((), ())), preferred_element_type=F32)


def tn(a, b):
    return lax.dot_general(a, b, (((0,), (0,)), ((), ())), preferred_element_type=F32)


def split(x):
    high = x.astype(BF16)
    return high, (x - high.astype(F32)).astype(BF16)


def iota(shape, dim):
    return lax.broadcasted_iota(jnp.int32, shape, dim)


def pool_matrix(rows, level):
    shape = (rows, rows << level)
    return jnp.where(iota(shape, 1) // (1 << level) == iota(shape, 0), 1.0, 0.0)


def pool_rows(x, level):
    mat = pool_matrix(x.shape[0] >> level, level).astype(BF16)
    high, low = split(x)
    return nn(mat, high) + nn(mat, low)


def spread_rows(x, level):
    mat = pool_matrix(x.shape[0], level).astype(BF16)
    high, low = split(x)
    return tn(mat, high) + tn(mat, low)


def low_lanes(shape):
    return iota(shape, 1) < HEAD


def key_side(kv, count):
    low = low_lanes(kv.shape)
    mean = pltpu.roll(kv / jnp.maximum(count, 1.0), HEAD, 1)
    mean_only = jnp.where(low, 0.0, mean)
    full = jnp.where(low, jnp.where(count > 0, 0.0, FAR_DEAD), mean)
    return full, mean_only


def value_side(kv, count):
    return jnp.where(low_lanes(kv.shape), count, kv)


def query_side(cq, scale):
    return jnp.where(low_lanes(cq.shape), 1.0, cq * scale)


def product3(a, b):
    ah, al = split(a)
    bh, bl = split(b)
    return nt(
        jnp.concatenate([ah, ah, al], axis=1), jnp.concatenate([bh, bl, bh], axis=1)
    )


def far_forward(query, key_full, value):
    scores = product3(query, key_full)
    top = jnp.max(scores, axis=1, keepdims=True)
    high, low = split(top)
    top = high.astype(F32) + low.astype(F32)
    weights = jnp.exp(scores - top).astype(BF16)
    vh, vl = split(value)
    out = nn(jnp.concatenate([weights, weights], axis=1), jnp.concatenate([vh, vl], axis=0))
    return weights, jnp.where(iota(out.shape, 1) == 0, top, out)


def far_backward(query, key_mean, value, count, weights, row_grad, scale):
    inner = product3(row_grad, value)
    dscore = (weights.astype(F32) * inner).astype(BF16)
    grad_query = nn(dscore, key_mean.astype(BF16)) * scale
    dk = tn(dscore, query.astype(BF16))
    dv = tn(weights, row_grad.astype(BF16))
    dk = pltpu.roll(dk, HEAD, 1) / jnp.maximum(count, 1.0)
    return grad_query, jnp.where(low_lanes(dv.shape), dk, dv)


def kernel(size, refs):
    bits = size.bit_length() - 1
    it = iter(refs)
    ids, q_ref, k_ref, v_ref, g_ref = (next(it) for _ in range(5))
    att_ref, gq_ref, gk_ref, gv_ref = (next(it) for _ in range(4))
    pall, kv_s, cq_s, wn_s, num_s, top_s, wf_s, fh_s, fl_s, rg_s = (next(it) for _ in range(10))
    gain_s, stat_s, sc_s, dq_s, dkv_s, dv_s = (next(it) for _ in range(6))
    sends = [next(it) for _ in range(bits)]
    recvs = [next(it) for _ in range(bits)]
    back_sends = [next(it) for _ in range(bits)]
    back_recvs = [next(it) for _ in range(bits)]
    send_sem, recv_sem, back_send_sem, back_recv_sem = (next(it) for _ in range(4))

    tokens = q_ref.shape[2]
    chunks = tokens // SPAN
    local_top = (tokens // BLOCK).bit_length() - 1
    scale = HEAD**-0.5
    me = lax.axis_index("seq")

    def flipped(m):
        out = me
        for bit in range(bits):
            if m >> bit & 1:
                out = out + (1 - 2 * lax.rem(lax.div(me, 1 << bit), 2)) * (1 << bit)
        return out

    barrier = pltpu.get_barrier_semaphore()
    for m in range(1, size):
        pl.semaphore_signal(
            barrier, inc=1, device_id={"seq": flipped(m)}, device_id_type=pl.DeviceIdType.MESH
        )

    start = {}
    at = 0
    for level in range(1, local_top + 1):
        start[level] = at
        at += tokens >> level
    prow = {}
    at = 0
    for level in range(1, local_top + 1):
        prow[level] = at
        at += SPAN >> level
    pooled_rows = at

    pieces = [pool_matrix(SPAN >> level, level) for level in range(1, local_top + 1)]
    pieces.append(jnp.zeros((SPAN - pooled_rows, SPAN), F32))
    pall[...] = jnp.concatenate(pieces, axis=0).astype(BF16)

    def span(p):
        return pl.ds(p * SPAN, SPAN)

    def level_rows(p, level):
        n = SPAN >> level
        return pl.ds(start[level] + p * n, n)

    def pool_slice(level):
        return pl.ds(prow[level], SPAN >> level)

    for p in range(chunks):
        cols = span(p)
        mask = jnp.where(ids[:, cols] != 0, 1.0, 0.0)
        maskh = jnp.broadcast_to(mask, (HEAD, SPAN))
        km = (k_ref[0, :, cols].astype(F32) * maskh).astype(BF16)
        vm = (v_ref[0, :, cols].astype(F32) * maskh).astype(BF16)
        x = jnp.concatenate([km, vm, maskh.astype(BF16), q_ref[0, :, cols]], axis=0)
        r = nt(pall[...], x)
        for level in range(1, local_top + 1):
            piece = r[prow[level] : prow[level] + (SPAN >> level)]
            kv_s[level_rows(p, level), :] = piece[:, :128]
            cq_s[level_rows(p, level), :] = piece[:, 128:]

    kv = kv_s[pl.ds(start[local_top], BLOCK), :]
    cq = cq_s[pl.ds(start[local_top], BLOCK), :]
    cross_query = []
    for b in range(bits):
        if b:
            kv, cq = pool_rows(kv, 1), pool_rows(cq, 1)
        cross_query.append(query_side(cq, scale * 2.0 ** -(local_top + b)))
        rows = BLOCK >> b
        sends[b][pl.ds(0, rows), :] = kv
        wide = cq if not b else jnp.concatenate([cq, jnp.zeros((BLOCK - rows, 128), F32)], axis=0)
        sends[b][pl.ds(rows, 8), :] = wide.T[:8]

    pl.semaphore_wait(barrier, size - 1)
    copies = []
    for m in range(1, size):
        b = m.bit_length() - 1
        copy = pltpu.make_async_remote_copy(
            src_ref=sends[b],
            dst_ref=recvs[b].at[lax.rem(me, 1 << b)],
            send_sem=send_sem.at[m - 1],
            recv_sem=recv_sem.at[m - 1],
            device_id={"seq": flipped(m)},
            device_id_type=pl.DeviceIdType.MESH,
        )
        copy.start()
        copies.append(copy)

    eye = iota((SPAN, SPAN), 0) == iota((SPAN, SPAN), 1)
    first = iota((16, SPAN), 0) == 0
    ones16 = jnp.where(first, 1.0, 0.0).astype(BF16)
    for p in range(chunks):
        cols = span(p)
        q = q_ref[0, :, cols]
        k = k_ref[0, :, cols]
        dead = jnp.where(ids[:, cols] != 0, 0.0, NEAR_DEAD)
        dead = jnp.where(first, dead, 0.0).astype(BF16)
        qf = q.astype(F32) * scale
        own = jnp.sum(qf * k.astype(F32), axis=0, keepdims=True)
        scores = tn(
            jnp.concatenate([k, dead], axis=0), jnp.concatenate([qf.astype(BF16), ones16], axis=0)
        )
        scores = jnp.where(eye, own, scores)
        top = jnp.max(scores, axis=0, keepdims=True)
        w = jnp.exp(scores - top).astype(BF16)
        wn_s[p] = w
        num_s[:, cols] = nn(jnp.concatenate([v_ref[0, :, cols], ones16], axis=0), w)
        top_s[:, cols] = jnp.broadcast_to(top, (8, SPAN))

    def far_operands(level, g):
        own = pl.ds(start[level] + g * BLOCK, BLOCK)
        other = pl.ds(start[level] + (g ^ 1) * BLOCK, BLOCK)
        kv = kv_s[other, :]
        count = cq_s[other, :]
        query = query_side(cq_s[own, :], scale * 2.0**-level)
        return own, other, kv, count, query

    for level in range(1, local_top):
        for g in range((tokens >> level) // BLOCK):
            own, other, kv, count, query = far_operands(level, g)
            w, f = far_forward(query, key_side(kv, count)[0], value_side(kv, count))
            wf_s[own, :] = w
            fh_s[own, :], fl_s[own, :] = split(f)

    for copy in copies:
        copy.wait_recv()
    cross = []
    for b in range(bits):
        rows = BLOCK >> b
        parts = [recvs[b][s] for s in range(1 << b)]
        kv = jnp.concatenate([x[:rows] for x in parts], axis=0)
        counts = []
        for x in parts:
            tile = jnp.concatenate([x[rows:]] * (BLOCK // 8), axis=0).T
            counts.append(tile[:rows])
        count = jnp.concatenate(counts, axis=0)
        key_full, key_mean = key_side(kv, count)
        value = value_side(kv, count)
        w, f = far_forward(cross_query[b], key_full, value)
        if b:
            f = spread_rows(f, b)
        cross.append((key_mean, value, count, w, f))
    best = cross[0][4][:, :1]
    for b in range(1, bits):
        best = jnp.maximum(best, cross[b][4][:, :1])
    gains = [jnp.exp(c[4][:, :1] - best) for c in cross]
    total = gains[0] * cross[0][4]
    for b in range(1, bits):
        total = total + gains[b] * cross[b][4]
    total = jnp.where(iota(total.shape, 1) == 0, best, total)
    whole = pl.ds(start[local_top], BLOCK)
    fh_s[whole, :], fl_s[whole, :] = split(total)

    row64 = iota((HEAD, SPAN), 0)
    for p in range(chunks):
        cols = span(p)
        wide = []
        for level in range(1, local_top + 1):
            rows = level_rows(p, level)
            mat = pall[pool_slice(level), :]
            wide.append(
                tn(
                    jnp.concatenate([fh_s[rows, :], fl_s[rows, :]], axis=0),
                    jnp.concatenate([mat, mat], axis=0),
                )
            )
        near_top = top_s[:1, cols]
        row_top = near_top
        for x in wide:
            row_top = jnp.maximum(row_top, x[:1])
        near_factor = jnp.exp(near_top - row_top)
        near = num_s[:, cols]
        numer = near_factor * near[:HEAD]
        denom = near_factor * near[HEAD : HEAD + 1]
        factors = []
        for x in wide:
            factor = jnp.exp(x[:1] - row_top)
            factors.append(factor)
            numer = numer + factor * x[HEAD:]
            denom = denom + factor * x[1:2]
        inverse = 1.0 / denom
        output = numer * inverse
        att_ref[0, :, cols] = output.astype(BF16)
        g = g_ref[0, :, cols].astype(F32)
        stat = jnp.sum(g * output, axis=0, keepdims=True)
        gain = near_factor * inverse
        gain_s[:, cols] = jnp.broadcast_to(gain, (8, SPAN))
        stat_s[:, cols] = jnp.broadcast_to(stat, (8, SPAN))
        sc_s[:, cols] = (gain * g).astype(BF16)
        for level in range(1, local_top + 1):
            far_gain = factors[level - 1] * inverse
            down = -(far_gain * stat)
            high = down.astype(BF16).astype(F32)
            head = jnp.where(row64 == 0, high, jnp.where(row64 == 1, down - high, 0.0))
            x = jnp.concatenate([head.astype(BF16), (far_gain * g).astype(BF16)], axis=0)
            rg_s[level_rows(p, level), :] = nt(pall[pool_slice(level), :], x)

    base = rg_s[whole, :]
    dq_total = None
    for b in range(bits):
        key_mean, value, count, w, _ = cross[b]
        row_grad = base * gains[b]
        if b:
            row_grad = pool_rows(row_grad, b)
        dq, dkv = far_backward(
            cross_query[b], key_mean, value, count, w, row_grad, scale * 2.0 ** -(local_top + b)
        )
        rows = BLOCK >> b
        for s in range(1 << b):
            back_sends[b][s] = dkv[s * rows : (s + 1) * rows]
        if b:
            dq = spread_rows(dq, b)
        dq_total = dq if dq_total is None else dq_total + dq
    dq_s[whole, :] = dq_total.astype(BF16)
    back_copies = []
    for m in range(1, size):
        b = m.bit_length() - 1
        copy = pltpu.make_async_remote_copy(
            src_ref=back_sends[b].at[lax.rem(flipped(m), 1 << b)],
            dst_ref=back_recvs[b].at[lax.rem(me, 1 << b)],
            send_sem=back_send_sem.at[m - 1],
            recv_sem=back_recv_sem.at[m - 1],
            device_id={"seq": flipped(m)},
            device_id_type=pl.DeviceIdType.MESH,
        )
        copy.start()
        back_copies.append(copy)

    for level in range(1, local_top):
        for g in range((tokens >> level) // BLOCK):
            own, other, kv, count, query = far_operands(level, g)
            dq, dkv = far_backward(
                query,
                key_side(kv, count)[1],
                value_side(kv, count),
                count,
                wf_s[own, :],
                rg_s[own, :],
                scale * 2.0**-level,
            )
            dq_s[own, :] = dq.astype(BF16)
            dkv_s[other, :] = dkv.astype(BF16)

    for p in range(chunks):
        cols = span(p)
        q, k, v, g = (r[0, :, cols] for r in (q_ref, k_ref, v_ref, g_ref))
        w = wn_s[p]
        dprob = tn(v, g)
        dscore = (
            w.astype(F32) * gain_s[:1, cols] * (dprob - stat_s[:1, cols])
        ).astype(BF16)
        num_s[:HEAD, cols] = nt(q, dscore) * scale
        dv_s[:, cols] = nt(sc_s[:, cols], w)
        gq = nn(k, dscore) * scale
        rows = [level_rows(p, level) for level in range(1, local_top + 1)]
        pad = jnp.zeros((SPAN - pooled_rows, 128), BF16)
        d = jnp.concatenate([dq_s[r, :] for r in rows] + [pad], axis=0)
        gq_ref[0, :, cols] = (gq + tn(d, pall[...])[HEAD:]).astype(BF16)

    for copy in back_copies:
        copy.wait_recv()
    acc = None
    for b in reversed(range(bits)):
        if acc is not None:
            acc = spread_rows(acc, 1)
        for s in range(1 << b):
            acc = back_recvs[b][s] if acc is None else acc + back_recvs[b][s]
    dkv_s[whole, :] = acc.astype(BF16)
    for p in range(chunks):
        cols = span(p)
        rows = [level_rows(p, level) for level in range(1, local_top + 1)]
        pad = jnp.zeros((SPAN - pooled_rows, 128), BF16)
        d = jnp.concatenate([dkv_s[r, :] for r in rows] + [pad], axis=0)
        far = tn(d, pall[...])
        valid = ids[:, cols] != 0
        far = jnp.where(valid, far, 0.0)
        gk_ref[0, :, cols] = (num_s[:HEAD, cols] + far[:HEAD]).astype(BF16)
        gv_ref[0, :, cols] = (dv_s[:, cols] + far[HEAD:]).astype(BF16)
    for copy in copies + back_copies:
        copy.wait_send()


def local(byte_ids, queries, key_states, values, cotangent):
    heads, width, tokens = queries.shape
    size = lax.axis_size("seq")
    bits = size.bit_length() - 1
    chunks = tokens // SPAN
    coarse = tokens - (tokens >> ((tokens // BLOCK).bit_length() - 1))
    vmem = pltpu.VMEM
    scratch = [
        vmem((SPAN, SPAN), BF16),
        vmem((coarse, 128), F32),
        vmem((coarse, 128), F32),
        vmem((chunks, SPAN, SPAN), BF16),
        vmem((HEAD + 16, tokens), F32),
        vmem((8, tokens), F32),
        vmem((coarse, 128), BF16),
        vmem((coarse, 128), BF16),
        vmem((coarse, 128), BF16),
        vmem((coarse, 128), F32),
        vmem((8, tokens), F32),
        vmem((8, tokens), F32),
        vmem((HEAD, tokens), BF16),
        vmem((coarse, 128), BF16),
        vmem((coarse, 128), BF16),
        vmem((HEAD, tokens), F32),
    ]
    scratch += [vmem(((BLOCK >> b) + 8, 128), F32) for b in range(bits)]
    scratch += [vmem((1 << b, (BLOCK >> b) + 8, 128), F32) for b in range(bits)]
    scratch += [vmem((1 << b, BLOCK >> b, 128), F32) for b in range(bits)] * 2
    scratch += [pltpu.SemaphoreType.DMA((size - 1,))] * 4
    out = jax.ShapeDtypeStruct(queries.shape, BF16)
    return pl.pallas_call(
        lambda *refs: kernel(size, refs),
        out_shape=(out,) * 4,
        in_specs=[pl.BlockSpec(memory_space=pltpu.VMEM)] * 5,
        out_specs=(pl.BlockSpec(memory_space=pltpu.VMEM),) * 4,
        scratch_shapes=scratch,
        compiler_params=pltpu.CompilerParams(
            collective_id=0, has_side_effects=True, vmem_limit_bytes=40 * 2**20
        ),
        cost_estimate=pl.CostEstimate(
            flops=2 * 10**9, bytes_accessed=3 * 10**6, transcendentals=10**6
        ),
    )(byte_ids.reshape(1, tokens), queries, key_states, values, cotangent)


def solution(mesh):
    wide = P("head", None, ("grp", "seq"))
    return jax.shard_map(
        local,
        mesh=mesh,
        in_specs=(P(("grp", "seq")), wide, wide, wide, wide),
        out_specs=(wide,) * 4,
        check_vma=False,
    )
```

```python
import jax
import jax.numpy as jnp
from jax import lax
from jax.experimental import pallas as pl
from jax.experimental.pallas import tpu as pltpu
from jax.sharding import PartitionSpec as P

HEAD = 64
VMEM_LIMIT = 62 * 2**20
BLOCK = 128
SPAN = 256
NEAR_DEAD = -(2.0**96)
FAR_DEAD = -(2.0**90)
F32 = jnp.float32
BF16 = jnp.bfloat16


def nn(a, b):
    return lax.dot_general(a, b, (((1,), (0,)), ((), ())), preferred_element_type=F32)


def nt(a, b):
    return lax.dot_general(a, b, (((1,), (1,)), ((), ())), preferred_element_type=F32)


def tn(a, b):
    return lax.dot_general(a, b, (((0,), (0,)), ((), ())), preferred_element_type=F32)


def split(x):
    high = x.astype(BF16)
    return high, (x - high.astype(F32)).astype(BF16)


def iota(shape, dim):
    return lax.broadcasted_iota(jnp.int32, shape, dim)


def pool_matrix(rows, level):
    shape = (rows, rows << level)
    return jnp.where(iota(shape, 1) // (1 << level) == iota(shape, 0), 1.0, 0.0)


def pool_rows(x, level):
    mat = pool_matrix(x.shape[0] >> level, level).astype(BF16)
    high, low = split(x)
    return nn(mat, high) + nn(mat, low)


def spread_rows(x, level):
    mat = pool_matrix(x.shape[0], level).astype(BF16)
    high, low = split(x)
    return tn(mat, high) + tn(mat, low)


def low_lanes(shape):
    return iota(shape, 1) < HEAD


def key_side(kv, count):
    low = low_lanes(kv.shape)
    mean = pltpu.roll(kv / jnp.maximum(count, 1.0), HEAD, 1)
    mean_only = jnp.where(low, 0.0, mean)
    full = jnp.where(low, jnp.where(count > 0, 0.0, FAR_DEAD), mean)
    return full, mean_only


def value_side(kv, count):
    return jnp.where(low_lanes(kv.shape), count, kv)


def query_side(cq, scale):
    return jnp.where(low_lanes(cq.shape), 1.0, cq * scale)


def product3(a, b):
    ah, al = split(a)
    bh, bl = split(b)
    return nt(
        jnp.concatenate([ah, ah, al], axis=1), jnp.concatenate([bh, bl, bh], axis=1)
    )


def far_forward(query, key_full, value):
    scores = product3(query, key_full)
    top = jnp.max(scores, axis=1, keepdims=True)
    high, low = split(top)
    top = high.astype(F32) + low.astype(F32)
    weights = jnp.exp(scores - top).astype(BF16)
    vh, vl = split(value)
    out = nn(jnp.concatenate([weights, weights], axis=1), jnp.concatenate([vh, vl], axis=0))
    return weights, jnp.where(iota(out.shape, 1) == 0, top, out)


def far_backward(query, key_mean, value, count, weights, row_grad, scale):
    inner = product3(row_grad, value)
    dscore = (weights.astype(F32) * inner).astype(BF16)
    grad_query = nn(dscore, key_mean.astype(BF16)) * scale
    dk = tn(dscore, query.astype(BF16))
    dv = tn(weights, row_grad.astype(BF16))
    dk = pltpu.roll(dk, HEAD, 1) / jnp.maximum(count, 1.0)
    return grad_query, jnp.where(low_lanes(dv.shape), dk, dv)


def kernel(size, refs):
    bits = size.bit_length() - 1
    it = iter(refs)
    sources = [next(it) for _ in range(5)]
    targets = [next(it) for _ in range(4)]
    pall, kv_s, cq_s, wn_s, num_s, top_s, wf_s, fh_s, fl_s, rg_s = (next(it) for _ in range(10))
    gain_s, stat_s, sc_s, dq_s, dkv_s, dv_s = (next(it) for _ in range(6))
    sends = [next(it) for _ in range(bits)]
    recvs = [next(it) for _ in range(bits)]
    back_sends = [next(it) for _ in range(bits)]
    back_recvs = [next(it) for _ in range(bits)]
    send_sem, recv_sem, back_send_sem, back_recv_sem = (next(it) for _ in range(4))
    ids, q_ref, k_ref, v_ref, g_ref = held = [next(it) for _ in range(5)]
    att_ref, gq_ref, gk_ref, gv_ref = results = [next(it) for _ in range(4)]
    in_sem, out_sem = next(it), next(it)
    stores = [pltpu.make_async_copy(x, y, out_sem.at[i]) for i, (x, y) in enumerate(zip(results, targets))]
    loads = [pltpu.make_async_copy(x, y, in_sem.at[i]) for i, (x, y) in enumerate(zip(sources, held))]
    for i in (0, 2, 3, 1, 4):
        loads[i].start()

    tokens = q_ref.shape[2]
    chunks = tokens // SPAN
    local_top = (tokens // BLOCK).bit_length() - 1
    scale = HEAD**-0.5
    me = lax.axis_index("seq")

    def flipped(m):
        out = me
        for bit in range(bits):
            if m >> bit & 1:
                out = out + (1 - 2 * lax.rem(lax.div(me, 1 << bit), 2)) * (1 << bit)
        return out

    barrier = pltpu.get_barrier_semaphore()
    for m in range(1, size):
        pl.semaphore_signal(
            barrier, inc=1, device_id={"seq": flipped(m)}, device_id_type=pl.DeviceIdType.MESH
        )

    start = {}
    at = 0
    for level in range(1, local_top + 1):
        start[level] = at
        at += tokens >> level
    prow = {}
    at = 0
    for level in range(1, local_top + 1):
        prow[level] = at
        at += SPAN >> level
    pooled_rows = at

    pieces = [pool_matrix(SPAN >> level, level) for level in range(1, local_top + 1)]
    pieces.append(jnp.zeros((SPAN - pooled_rows, SPAN), F32))
    pall[...] = jnp.concatenate(pieces, axis=0).astype(BF16)

    def span(p):
        return pl.ds(p * SPAN, SPAN)

    def level_rows(p, level):
        n = SPAN >> level
        return pl.ds(start[level] + p * n, n)

    def pool_slice(level):
        return pl.ds(prow[level], SPAN >> level)

    for i in range(4):
        loads[i].wait()

    for p in range(chunks):
        cols = span(p)
        mask = jnp.where(ids[:, cols] != 0, 1.0, 0.0)
        maskh = jnp.broadcast_to(mask, (HEAD, SPAN))
        km = (k_ref[0, :, cols].astype(F32) * maskh).astype(BF16)
        vm = (v_ref[0, :, cols].astype(F32) * maskh).astype(BF16)
        x = jnp.concatenate([km, vm, maskh.astype(BF16), q_ref[0, :, cols]], axis=0)
        r = nt(pall[...], x)
        for level in range(1, local_top + 1):
            piece = r[prow[level] : prow[level] + (SPAN >> level)]
            kv_s[level_rows(p, level), :] = piece[:, :128]
            cq_s[level_rows(p, level), :] = piece[:, 128:]

    kv = kv_s[pl.ds(start[local_top], BLOCK), :]
    cq = cq_s[pl.ds(start[local_top], BLOCK), :]
    cross_query = []
    for b in range(bits):
        if b:
            kv, cq = pool_rows(kv, 1), pool_rows(cq, 1)
        cross_query.append(query_side(cq, scale * 2.0 ** -(local_top + b)))
        rows = BLOCK >> b
        sends[b][pl.ds(0, rows), :] = kv
        wide = cq if not b else jnp.concatenate([cq, jnp.zeros((BLOCK - rows, 128), F32)], axis=0)
        sends[b][pl.ds(rows, 8), :] = wide.T[:8]

    pl.semaphore_wait(barrier, size - 1)
    copies = []
    for m in range(1, size):
        b = m.bit_length() - 1
        copy = pltpu.make_async_remote_copy(
            src_ref=sends[b],
            dst_ref=recvs[b].at[lax.rem(me, 1 << b)],
            send_sem=send_sem.at[m - 1],
            recv_sem=recv_sem.at[m - 1],
            device_id={"seq": flipped(m)},
            device_id_type=pl.DeviceIdType.MESH,
        )
        copy.start()
        copies.append(copy)

    eye = iota((SPAN, SPAN), 0) == iota((SPAN, SPAN), 1)
    first = iota((16, SPAN), 0) == 0
    ones16 = jnp.where(first, 1.0, 0.0).astype(BF16)
    for p in range(chunks):
        cols = span(p)
        q = q_ref[0, :, cols]
        k = k_ref[0, :, cols]
        dead = jnp.where(ids[:, cols] != 0, 0.0, NEAR_DEAD)
        dead = jnp.where(first, dead, 0.0).astype(BF16)
        qf = q.astype(F32) * scale
        own = jnp.sum(qf * k.astype(F32), axis=0, keepdims=True)
        scores = tn(
            jnp.concatenate([k, dead], axis=0), jnp.concatenate([qf.astype(BF16), ones16], axis=0)
        )
        scores = jnp.where(eye, own, scores)
        top = jnp.max(scores, axis=0, keepdims=True)
        w = jnp.exp(scores - top).astype(BF16)
        wn_s[p] = w
        num_s[:, cols] = nn(jnp.concatenate([v_ref[0, :, cols], ones16], axis=0), w)
        top_s[:, cols] = jnp.broadcast_to(top, (8, SPAN))

    def far_operands(level, g):
        own = pl.ds(start[level] + g * BLOCK, BLOCK)
        other = pl.ds(start[level] + (g ^ 1) * BLOCK, BLOCK)
        kv = kv_s[other, :]
        count = cq_s[other, :]
        query = query_side(cq_s[own, :], scale * 2.0**-level)
        return own, other, kv, count, query

    for level in range(1, local_top):
        for g in range((tokens >> level) // BLOCK):
            own, other, kv, count, query = far_operands(level, g)
            w, f = far_forward(query, key_side(kv, count)[0], value_side(kv, count))
            wf_s[own, :] = w
            fh_s[own, :], fl_s[own, :] = split(f)

    for copy in copies:
        copy.wait_recv()
    cross = []
    for b in range(bits):
        rows = BLOCK >> b
        parts = [recvs[b][s] for s in range(1 << b)]
        kv = jnp.concatenate([x[:rows] for x in parts], axis=0)
        counts = []
        for x in parts:
            tile = jnp.concatenate([x[rows:]] * (BLOCK // 8), axis=0).T
            counts.append(tile[:rows])
        count = jnp.concatenate(counts, axis=0)
        key_full, key_mean = key_side(kv, count)
        value = value_side(kv, count)
        w, f = far_forward(cross_query[b], key_full, value)
        if b:
            f = spread_rows(f, b)
        cross.append((key_mean, value, count, w, f))
    best = cross[0][4][:, :1]
    for b in range(1, bits):
        best = jnp.maximum(best, cross[b][4][:, :1])
    gains = [jnp.exp(c[4][:, :1] - best) for c in cross]
    total = gains[0] * cross[0][4]
    for b in range(1, bits):
        total = total + gains[b] * cross[b][4]
    total = jnp.where(iota(total.shape, 1) == 0, best, total)
    whole = pl.ds(start[local_top], BLOCK)
    fh_s[whole, :], fl_s[whole, :] = split(total)

    loads[4].wait()

    row64 = iota((HEAD, SPAN), 0)
    for p in range(chunks):
        cols = span(p)
        wide = []
        for level in range(1, local_top + 1):
            rows = level_rows(p, level)
            mat = pall[pool_slice(level), :]
            wide.append(
                tn(
                    jnp.concatenate([fh_s[rows, :], fl_s[rows, :]], axis=0),
                    jnp.concatenate([mat, mat], axis=0),
                )
            )
        near_top = top_s[:1, cols]
        row_top = near_top
        for x in wide:
            row_top = jnp.maximum(row_top, x[:1])
        near_factor = jnp.exp(near_top - row_top)
        near = num_s[:, cols]
        numer = near_factor * near[:HEAD]
        denom = near_factor * near[HEAD : HEAD + 1]
        factors = []
        for x in wide:
            factor = jnp.exp(x[:1] - row_top)
            factors.append(factor)
            numer = numer + factor * x[HEAD:]
            denom = denom + factor * x[1:2]
        inverse = 1.0 / denom
        output = numer * inverse
        att_ref[0, :, cols] = output.astype(BF16)
        g = g_ref[0, :, cols].astype(F32)
        stat = jnp.sum(g * output, axis=0, keepdims=True)
        gain = near_factor * inverse
        gain_s[:, cols] = jnp.broadcast_to(gain, (8, SPAN))
        stat_s[:, cols] = jnp.broadcast_to(stat, (8, SPAN))
        sc_s[:, cols] = (gain * g).astype(BF16)
        for level in range(1, local_top + 1):
            far_gain = factors[level - 1] * inverse
            down = -(far_gain * stat)
            high = down.astype(BF16).astype(F32)
            head = jnp.where(row64 == 0, high, jnp.where(row64 == 1, down - high, 0.0))
            x = jnp.concatenate([head.astype(BF16), (far_gain * g).astype(BF16)], axis=0)
            rg_s[level_rows(p, level), :] = nt(pall[pool_slice(level), :], x)

    stores[0].start()

    base = rg_s[whole, :]
    dq_total = None
    for b in range(bits):
        key_mean, value, count, w, _ = cross[b]
        row_grad = base * gains[b]
        if b:
            row_grad = pool_rows(row_grad, b)
        dq, dkv = far_backward(
            cross_query[b], key_mean, value, count, w, row_grad, scale * 2.0 ** -(local_top + b)
        )
        rows = BLOCK >> b
        for s in range(1 << b):
            back_sends[b][s] = dkv[s * rows : (s + 1) * rows]
        if b:
            dq = spread_rows(dq, b)
        dq_total = dq if dq_total is None else dq_total + dq
    dq_s[whole, :] = dq_total.astype(BF16)
    back_copies = []
    for m in range(1, size):
        b = m.bit_length() - 1
        copy = pltpu.make_async_remote_copy(
            src_ref=back_sends[b].at[lax.rem(flipped(m), 1 << b)],
            dst_ref=back_recvs[b].at[lax.rem(me, 1 << b)],
            send_sem=back_send_sem.at[m - 1],
            recv_sem=back_recv_sem.at[m - 1],
            device_id={"seq": flipped(m)},
            device_id_type=pl.DeviceIdType.MESH,
        )
        copy.start()
        back_copies.append(copy)

    for level in range(1, local_top):
        for g in range((tokens >> level) // BLOCK):
            own, other, kv, count, query = far_operands(level, g)
            dq, dkv = far_backward(
                query,
                key_side(kv, count)[1],
                value_side(kv, count),
                count,
                wf_s[own, :],
                rg_s[own, :],
                scale * 2.0**-level,
            )
            dq_s[own, :] = dq.astype(BF16)
            dkv_s[other, :] = dkv.astype(BF16)

    for p in range(chunks):
        cols = span(p)
        q, k, v, g = (r[0, :, cols] for r in (q_ref, k_ref, v_ref, g_ref))
        w = wn_s[p]
        dprob = tn(v, g)
        dscore = (
            w.astype(F32) * gain_s[:1, cols] * (dprob - stat_s[:1, cols])
        ).astype(BF16)
        num_s[:HEAD, cols] = nt(q, dscore) * scale
        dv_s[:, cols] = nt(sc_s[:, cols], w)
        gq = nn(k, dscore) * scale
        rows = [level_rows(p, level) for level in range(1, local_top + 1)]
        pad = jnp.zeros((SPAN - pooled_rows, 128), BF16)
        d = jnp.concatenate([dq_s[r, :] for r in rows] + [pad], axis=0)
        gq_ref[0, :, cols] = (gq + tn(d, pall[...])[HEAD:]).astype(BF16)

    stores[1].start()
    for copy in back_copies:
        copy.wait_recv()
    acc = None
    for b in reversed(range(bits)):
        if acc is not None:
            acc = spread_rows(acc, 1)
        for s in range(1 << b):
            acc = back_recvs[b][s] if acc is None else acc + back_recvs[b][s]
    dkv_s[whole, :] = acc.astype(BF16)
    for p in range(chunks):
        cols = span(p)
        rows = [level_rows(p, level) for level in range(1, local_top + 1)]
        pad = jnp.zeros((SPAN - pooled_rows, 128), BF16)
        d = jnp.concatenate([dkv_s[r, :] for r in rows] + [pad], axis=0)
        far = tn(d, pall[...])
        valid = ids[:, cols] != 0
        far = jnp.where(valid, far, 0.0)
        gk_ref[0, :, cols] = (num_s[:HEAD, cols] + far[:HEAD]).astype(BF16)
        gv_ref[0, :, cols] = (dv_s[:, cols] + far[HEAD:]).astype(BF16)
    stores[2].start()
    stores[3].start()
    for copy in copies + back_copies:
        copy.wait_send()
    for store in stores:
        store.wait()


def flush(*refs):
    sem = refs[8]
    copies = [pltpu.make_async_copy(refs[i], refs[4 + i], sem.at[i]) for i in range(4)]
    for copy in copies:
        copy.start()
    for copy in copies:
        copy.wait()


def local(byte_ids, queries, key_states, values, cotangent):
    heads, width, tokens = queries.shape
    size = lax.axis_size("seq")
    bits = size.bit_length() - 1
    chunks = tokens // SPAN
    coarse = tokens - (tokens >> ((tokens // BLOCK).bit_length() - 1))
    vmem = pltpu.VMEM
    scratch = [
        vmem((SPAN, SPAN), BF16),
        vmem((coarse, 128), F32),
        vmem((coarse, 128), F32),
        vmem((chunks, SPAN, SPAN), BF16),
        vmem((HEAD + 16, tokens), F32),
        vmem((8, tokens), F32),
        vmem((coarse, 128), BF16),
        vmem((coarse, 128), BF16),
        vmem((coarse, 128), BF16),
        vmem((coarse, 128), F32),
        vmem((8, tokens), F32),
        vmem((8, tokens), F32),
        vmem((HEAD, tokens), BF16),
        vmem((coarse, 128), BF16),
        vmem((coarse, 128), BF16),
        vmem((HEAD, tokens), F32),
    ]
    scratch += [vmem(((BLOCK >> b) + 8, 128), F32) for b in range(bits)]
    scratch += [vmem((1 << b, (BLOCK >> b) + 8, 128), F32) for b in range(bits)]
    scratch += [vmem((1 << b, BLOCK >> b, 128), F32) for b in range(bits)] * 2
    scratch += [pltpu.SemaphoreType.DMA((size - 1,))] * 4
    scratch += [vmem((1, tokens), jnp.int32)] + [vmem(queries.shape, BF16)] * 8
    scratch += [pltpu.SemaphoreType.DMA((5,)), pltpu.SemaphoreType.DMA((4,))]
    out = jax.ShapeDtypeStruct(queries.shape, BF16)
    results = pl.pallas_call(
        lambda *refs: kernel(size, refs),
        out_shape=(out,) * 4,
        in_specs=[pl.BlockSpec(memory_space=pltpu.HBM)] * 5,
        out_specs=(pl.BlockSpec(memory_space=pltpu.HBM),) * 4,
        scratch_shapes=scratch,
        compiler_params=pltpu.CompilerParams(
            collective_id=0, has_side_effects=True, vmem_limit_bytes=VMEM_LIMIT
        ),
        cost_estimate=pl.CostEstimate(
            flops=2 * 10**9, bytes_accessed=3 * 10**6, transcendentals=10**6
        ),
    )(byte_ids.reshape(1, tokens), queries, key_states, values, cotangent)
    return pl.pallas_call(
        flush,
        out_shape=(out,) * 4,
        in_specs=[pl.BlockSpec(memory_space=pltpu.HBM)] * 4,
        out_specs=(pl.BlockSpec(memory_space=pltpu.HBM),) * 4,
        scratch_shapes=[pltpu.SemaphoreType.DMA((4,))],
        compiler_params=pltpu.CompilerParams(vmem_limit_bytes=VMEM_LIMIT),
    )(*results)


def solution(mesh):
    wide = P("head", None, ("grp", "seq"))
    return jax.shard_map(
        local,
        mesh=mesh,
        in_specs=(P(("grp", "seq")), wide, wide, wide, wide),
        out_specs=(wide,) * 4,
        check_vma=False,
    )
```

```python
import jax
import jax.numpy as jnp
from jax import lax
from jax.experimental import pallas as pl
from jax.experimental.pallas import tpu as pltpu
from jax.sharding import PartitionSpec as P

HEAD = 64
VMEM_LIMIT = 62 * 2**20
BLOCK = 128
SPAN = 256
NEAR_DEAD = -(2.0**96)
FAR_DEAD = -(2.0**90)
F32 = jnp.float32
BF16 = jnp.bfloat16


def nn(a, b):
    return lax.dot_general(a, b, (((1,), (0,)), ((), ())), preferred_element_type=F32)


def nt(a, b):
    return lax.dot_general(a, b, (((1,), (1,)), ((), ())), preferred_element_type=F32)


def tn(a, b):
    return lax.dot_general(a, b, (((0,), (0,)), ((), ())), preferred_element_type=F32)


def split(x):
    high = x.astype(BF16)
    return high, (x - high.astype(F32)).astype(BF16)


def iota(shape, dim):
    return lax.broadcasted_iota(jnp.int32, shape, dim)


def pool_matrix(rows, level):
    shape = (rows, rows << level)
    return jnp.where(iota(shape, 1) // (1 << level) == iota(shape, 0), 1.0, 0.0)


def pool_rows(x, level):
    mat = pool_matrix(x.shape[0] >> level, level).astype(BF16)
    high, low = split(x)
    return nn(mat, high) + nn(mat, low)


def spread_rows(x, level):
    mat = pool_matrix(x.shape[0], level).astype(BF16)
    high, low = split(x)
    return tn(mat, high) + tn(mat, low)


def low_lanes(shape):
    return iota(shape, 1) < HEAD


def key_side(kv, count):
    low = low_lanes(kv.shape)
    mean = pltpu.roll(kv / jnp.maximum(count, 1.0), HEAD, 1)
    mean_only = jnp.where(low, 0.0, mean)
    full = jnp.where(low, jnp.where(count > 0, 0.0, FAR_DEAD), mean)
    return full, mean_only


def value_side(kv, count):
    return jnp.where(low_lanes(kv.shape), count, kv)


def query_side(cq, scale):
    return jnp.where(low_lanes(cq.shape), 1.0, cq * scale)


def product3(a, b):
    ah, al = split(a)
    bh, bl = split(b)
    return nt(
        jnp.concatenate([ah, ah, al], axis=1), jnp.concatenate([bh, bl, bh], axis=1)
    )


def far_forward(query, key_full, value):
    scores = product3(query, key_full)
    top = jnp.max(scores, axis=1, keepdims=True)
    high, low = split(top)
    top = high.astype(F32) + low.astype(F32)
    weights = jnp.exp(scores - top).astype(BF16)
    vh, vl = split(value)
    out = nn(jnp.concatenate([weights, weights], axis=1), jnp.concatenate([vh, vl], axis=0))
    return weights, jnp.where(iota(out.shape, 1) == 0, top, out)


def far_backward(query, key_mean, value, count, weights, row_grad, scale):
    inner = product3(row_grad, value)
    dscore = (weights.astype(F32) * inner).astype(BF16)
    grad_query = nn(dscore, key_mean.astype(BF16)) * scale
    dk = tn(dscore, query.astype(BF16))
    dv = tn(weights, row_grad.astype(BF16))
    dk = pltpu.roll(dk, HEAD, 1) / jnp.maximum(count, 1.0)
    return grad_query, jnp.where(low_lanes(dv.shape), dk, dv)


def kernel(size, refs):
    bits = size.bit_length() - 1
    it = iter(refs)
    sources = [next(it) for _ in range(5)]
    targets = [next(it) for _ in range(4)]
    pall, kv_s, cq_s, wn_s, num_s, top_s, wf_s, fh_s, fl_s, rg_s = (next(it) for _ in range(10))
    gain_s, stat_s, sc_s, dq_s, dkv_s, dv_s = (next(it) for _ in range(6))
    sends = [next(it) for _ in range(bits)]
    recvs = [next(it) for _ in range(bits)]
    back_sends = [next(it) for _ in range(bits)]
    back_recvs = [next(it) for _ in range(bits)]
    send_sem, recv_sem, back_send_sem, back_recv_sem = (next(it) for _ in range(4))
    ids, q_ref, k_ref, v_ref, g_ref = held = [next(it) for _ in range(5)]
    att_ref, gq_ref, gk_ref, gv_ref = results = [next(it) for _ in range(4)]
    in_sem, out_sem = next(it), next(it)
    stores = [pltpu.make_async_copy(x, y, out_sem.at[i]) for i, (x, y) in enumerate(zip(results, targets))]
    loads = [pltpu.make_async_copy(x, y, in_sem.at[i]) for i, (x, y) in enumerate(zip(sources, held))]
    for i in (0, 2, 3, 1, 4):
        loads[i].start()

    tokens = q_ref.shape[2]
    chunks = tokens // SPAN
    local_top = (tokens // BLOCK).bit_length() - 1
    scale = HEAD**-0.5
    me = lax.axis_index("seq")

    def flipped(m):
        out = me
        for bit in range(bits):
            if m >> bit & 1:
                out = out + (1 - 2 * lax.rem(lax.div(me, 1 << bit), 2)) * (1 << bit)
        return out

    barrier = pltpu.get_barrier_semaphore()
    for m in range(1, size):
        pl.semaphore_signal(
            barrier, inc=1, device_id={"seq": flipped(m)}, device_id_type=pl.DeviceIdType.MESH
        )

    start = {}
    at = 0
    for level in range(1, local_top + 1):
        start[level] = at
        at += tokens >> level
    prow = {}
    at = 0
    for level in range(1, local_top + 1):
        prow[level] = at
        at += SPAN >> level
    pooled_rows = at

    pieces = [pool_matrix(SPAN >> level, level) for level in range(1, local_top + 1)]
    pieces.append(jnp.zeros((SPAN - pooled_rows, SPAN), F32))
    pall[...] = jnp.concatenate(pieces, axis=0).astype(BF16)

    def span(p):
        return pl.ds(p * SPAN, SPAN)

    def level_rows(p, level):
        n = SPAN >> level
        return pl.ds(start[level] + p * n, n)

    def pool_slice(level):
        return pl.ds(prow[level], SPAN >> level)

    for i in range(4):
        loads[i].wait()

    for p in range(chunks):
        cols = span(p)
        mask = jnp.where(ids[:, cols] != 0, 1.0, 0.0)
        maskh = jnp.broadcast_to(mask, (HEAD, SPAN))
        km = (k_ref[0, :, cols].astype(F32) * maskh).astype(BF16)
        vm = (v_ref[0, :, cols].astype(F32) * maskh).astype(BF16)
        x = jnp.concatenate([km, vm, maskh.astype(BF16), q_ref[0, :, cols]], axis=0)
        r = nt(pall[...], x)
        for level in range(1, local_top + 1):
            piece = r[prow[level] : prow[level] + (SPAN >> level)]
            kv_s[level_rows(p, level), :] = piece[:, :128]
            cq_s[level_rows(p, level), :] = piece[:, 128:]

    kv = kv_s[pl.ds(start[local_top], BLOCK), :]
    cq = cq_s[pl.ds(start[local_top], BLOCK), :]
    cross_query = []
    for b in range(bits):
        if b:
            kv, cq = pool_rows(kv, 1), pool_rows(cq, 1)
        cross_query.append(query_side(cq, scale * 2.0 ** -(local_top + b)))
        rows = BLOCK >> b
        sends[b][pl.ds(0, rows), :] = kv
        wide = cq if not b else jnp.concatenate([cq, jnp.zeros((BLOCK - rows, 128), F32)], axis=0)
        sends[b][pl.ds(rows, 8), :] = wide.T[:8]

    pl.semaphore_wait(barrier, size - 1)
    copies = []
    for m in range(1, size):
        b = m.bit_length() - 1
        copy = pltpu.make_async_remote_copy(
            src_ref=sends[b],
            dst_ref=recvs[b].at[lax.rem(me, 1 << b)],
            send_sem=send_sem.at[m - 1],
            recv_sem=recv_sem.at[m - 1],
            device_id={"seq": flipped(m)},
            device_id_type=pl.DeviceIdType.MESH,
        )
        copy.start()
        copies.append(copy)

    eye = iota((SPAN, SPAN), 0) == iota((SPAN, SPAN), 1)
    first = iota((16, SPAN), 0) == 0
    ones16 = jnp.where(first, 1.0, 0.0).astype(BF16)
    for p in range(chunks):
        cols = span(p)
        q = q_ref[0, :, cols]
        k = k_ref[0, :, cols]
        dead = jnp.where(ids[:, cols] != 0, 0.0, NEAR_DEAD)
        dead = jnp.where(first, dead, 0.0).astype(BF16)
        qf = q.astype(F32) * scale
        own = jnp.sum(qf * k.astype(F32), axis=0, keepdims=True)
        scores = tn(
            jnp.concatenate([k, dead], axis=0), jnp.concatenate([qf.astype(BF16), ones16], axis=0)
        )
        scores = jnp.where(eye, own, scores)
        top = jnp.max(scores, axis=0, keepdims=True)
        w = jnp.exp(scores - top).astype(BF16)
        wn_s[p] = w
        num_s[:, cols] = nn(jnp.concatenate([v_ref[0, :, cols], ones16], axis=0), w)
        top_s[:, cols] = jnp.broadcast_to(top, (8, SPAN))

    def far_operands(level, g):
        own = pl.ds(start[level] + g * BLOCK, BLOCK)
        other = pl.ds(start[level] + (g ^ 1) * BLOCK, BLOCK)
        kv = kv_s[other, :]
        count = cq_s[other, :]
        query = query_side(cq_s[own, :], scale * 2.0**-level)
        return own, other, kv, count, query

    for level in range(1, local_top):
        for g in range((tokens >> level) // BLOCK):
            own, other, kv, count, query = far_operands(level, g)
            w, f = far_forward(query, key_side(kv, count)[0], value_side(kv, count))
            wf_s[own, :] = w
            fh_s[own, :], fl_s[own, :] = split(f)

    for copy in copies:
        copy.wait_recv()
    cross = []
    for b in range(bits):
        rows = BLOCK >> b
        parts = [recvs[b][s] for s in range(1 << b)]
        kv = jnp.concatenate([x[:rows] for x in parts], axis=0)
        counts = []
        for x in parts:
            tile = jnp.concatenate([x[rows:]] * (BLOCK // 8), axis=0).T
            counts.append(tile[:rows])
        count = jnp.concatenate(counts, axis=0)
        key_full, key_mean = key_side(kv, count)
        value = value_side(kv, count)
        w, f = far_forward(cross_query[b], key_full, value)
        if b:
            f = spread_rows(f, b)
        cross.append((key_mean, value, count, w, f))
    best = cross[0][4][:, :1]
    for b in range(1, bits):
        best = jnp.maximum(best, cross[b][4][:, :1])
    gains = [jnp.exp(c[4][:, :1] - best) for c in cross]
    total = gains[0] * cross[0][4]
    for b in range(1, bits):
        total = total + gains[b] * cross[b][4]
    total = jnp.where(iota(total.shape, 1) == 0, best, total)
    whole = pl.ds(start[local_top], BLOCK)
    fh_s[whole, :], fl_s[whole, :] = split(total)

    loads[4].wait()

    row64 = iota((HEAD, SPAN), 0)
    for p in range(chunks):
        cols = span(p)
        wide = []
        for level in range(1, local_top + 1):
            rows = level_rows(p, level)
            mat = pall[pool_slice(level), :]
            wide.append(
                tn(
                    jnp.concatenate([fh_s[rows, :], fl_s[rows, :]], axis=0),
                    jnp.concatenate([mat, mat], axis=0),
                )
            )
        near_top = top_s[:1, cols]
        row_top = near_top
        for x in wide:
            row_top = jnp.maximum(row_top, x[:1])
        near_factor = jnp.exp(near_top - row_top)
        near = num_s[:, cols]
        numer = near_factor * near[:HEAD]
        denom = near_factor * near[HEAD : HEAD + 1]
        factors = []
        for x in wide:
            factor = jnp.exp(x[:1] - row_top)
            factors.append(factor)
            numer = numer + factor * x[HEAD:]
            denom = denom + factor * x[1:2]
        inverse = 1.0 / denom
        output = numer * inverse
        att_ref[0, :, cols] = output.astype(BF16)
        g = g_ref[0, :, cols].astype(F32)
        stat = jnp.sum(g * output, axis=0, keepdims=True)
        gain = near_factor * inverse
        gain_s[:, cols] = jnp.broadcast_to(gain, (8, SPAN))
        stat_s[:, cols] = jnp.broadcast_to(stat, (8, SPAN))
        sc_s[:, cols] = (gain * g).astype(BF16)
        for level in range(1, local_top + 1):
            far_gain = factors[level - 1] * inverse
            down = -(far_gain * stat)
            high = down.astype(BF16).astype(F32)
            head = jnp.where(row64 == 0, high, jnp.where(row64 == 1, down - high, 0.0))
            x = jnp.concatenate([head.astype(BF16), (far_gain * g).astype(BF16)], axis=0)
            rg_s[level_rows(p, level), :] = nt(pall[pool_slice(level), :], x)

    stores[0].start()

    base = rg_s[whole, :]
    dq_total = None
    for b in range(bits):
        key_mean, value, count, w, _ = cross[b]
        row_grad = base * gains[b]
        if b:
            row_grad = pool_rows(row_grad, b)
        dq, dkv = far_backward(
            cross_query[b], key_mean, value, count, w, row_grad, scale * 2.0 ** -(local_top + b)
        )
        rows = BLOCK >> b
        for s in range(1 << b):
            back_sends[b][s] = dkv[s * rows : (s + 1) * rows]
        if b:
            dq = spread_rows(dq, b)
        dq_total = dq if dq_total is None else dq_total + dq
    dq_s[whole, :] = dq_total.astype(BF16)
    back_copies = []
    for m in range(1, size):
        b = m.bit_length() - 1
        copy = pltpu.make_async_remote_copy(
            src_ref=back_sends[b].at[lax.rem(flipped(m), 1 << b)],
            dst_ref=back_recvs[b].at[lax.rem(me, 1 << b)],
            send_sem=back_send_sem.at[m - 1],
            recv_sem=back_recv_sem.at[m - 1],
            device_id={"seq": flipped(m)},
            device_id_type=pl.DeviceIdType.MESH,
        )
        copy.start()
        back_copies.append(copy)

    for level in range(1, local_top):
        for g in range((tokens >> level) // BLOCK):
            own, other, kv, count, query = far_operands(level, g)
            dq, dkv = far_backward(
                query,
                key_side(kv, count)[1],
                value_side(kv, count),
                count,
                wf_s[own, :],
                rg_s[own, :],
                scale * 2.0**-level,
            )
            dq_s[own, :] = dq.astype(BF16)
            dkv_s[other, :] = dkv.astype(BF16)

    for p in range(chunks):
        cols = span(p)
        q, k, v, g = (r[0, :, cols] for r in (q_ref, k_ref, v_ref, g_ref))
        w = wn_s[p]
        dprob = tn(v, g)
        dscore = (
            w.astype(F32) * gain_s[:1, cols] * (dprob - stat_s[:1, cols])
        ).astype(BF16)
        num_s[:HEAD, cols] = nt(q, dscore) * scale
        dv_s[:, cols] = nt(sc_s[:, cols], w)
        gq = nn(k, dscore) * scale
        rows = [level_rows(p, level) for level in range(1, local_top + 1)]
        pad = jnp.zeros((SPAN - pooled_rows, 128), BF16)
        d = jnp.concatenate([dq_s[r, :] for r in rows] + [pad], axis=0)
        gq_ref[0, :, cols] = (gq + tn(d, pall[...])[HEAD:]).astype(BF16)

    stores[1].start()
    for copy in back_copies:
        copy.wait_recv()
    acc = None
    for b in reversed(range(bits)):
        if acc is not None:
            acc = spread_rows(acc, 1)
        for s in range(1 << b):
            acc = back_recvs[b][s] if acc is None else acc + back_recvs[b][s]
    dkv_s[whole, :] = acc.astype(BF16)
    for p in range(chunks):
        cols = span(p)
        rows = [level_rows(p, level) for level in range(1, local_top + 1)]
        pad = jnp.zeros((SPAN - pooled_rows, 128), BF16)
        d = jnp.concatenate([dkv_s[r, :] for r in rows] + [pad], axis=0)
        far = tn(d, pall[...])
        valid = ids[:, cols] != 0
        far = jnp.where(valid, far, 0.0)
        gk_ref[0, :, cols] = (num_s[:HEAD, cols] + far[:HEAD]).astype(BF16)
        gv_ref[0, :, cols] = (dv_s[:, cols] + far[HEAD:]).astype(BF16)
    stores[2].start()
    stores[3].start()
    for copy in copies + back_copies:
        copy.wait_send()
    for store in stores:
        store.wait()


def flush(*refs):
    sem = refs[12]
    loads = [pltpu.make_async_copy(refs[i], refs[8 + i], sem.at[i]) for i in range(4)]
    stores = [pltpu.make_async_copy(refs[8 + i], refs[4 + i], sem.at[4 + i]) for i in range(4)]
    for load in loads:
        load.start()
    for load, store in zip(loads, stores):
        load.wait()
        store.start()
    for store in stores:
        store.wait()


def local(byte_ids, queries, key_states, values, cotangent):
    heads, width, tokens = queries.shape
    size = lax.axis_size("seq")
    bits = size.bit_length() - 1
    chunks = tokens // SPAN
    coarse = tokens - (tokens >> ((tokens // BLOCK).bit_length() - 1))
    vmem = pltpu.VMEM
    scratch = [
        vmem((SPAN, SPAN), BF16),
        vmem((coarse, 128), F32),
        vmem((coarse, 128), F32),
        vmem((chunks, SPAN, SPAN), BF16),
        vmem((HEAD + 16, tokens), F32),
        vmem((8, tokens), F32),
        vmem((coarse, 128), BF16),
        vmem((coarse, 128), BF16),
        vmem((coarse, 128), BF16),
        vmem((coarse, 128), F32),
        vmem((8, tokens), F32),
        vmem((8, tokens), F32),
        vmem((HEAD, tokens), BF16),
        vmem((coarse, 128), BF16),
        vmem((coarse, 128), BF16),
        vmem((HEAD, tokens), F32),
    ]
    scratch += [vmem(((BLOCK >> b) + 8, 128), F32) for b in range(bits)]
    scratch += [vmem((1 << b, (BLOCK >> b) + 8, 128), F32) for b in range(bits)]
    scratch += [vmem((1 << b, BLOCK >> b, 128), F32) for b in range(bits)] * 2
    scratch += [pltpu.SemaphoreType.DMA((size - 1,))] * 4
    scratch += [vmem((1, tokens), jnp.int32)] + [vmem(queries.shape, BF16)] * 8
    scratch += [pltpu.SemaphoreType.DMA((5,)), pltpu.SemaphoreType.DMA((4,))]
    out = jax.ShapeDtypeStruct(queries.shape, BF16)
    results = pl.pallas_call(
        lambda *refs: kernel(size, refs),
        out_shape=(out,) * 4,
        in_specs=[pl.BlockSpec(memory_space=pltpu.HBM)] * 5,
        out_specs=(pl.BlockSpec(memory_space=pltpu.HBM),) * 4,
        scratch_shapes=scratch,
        compiler_params=pltpu.CompilerParams(
            collective_id=0, has_side_effects=True, vmem_limit_bytes=VMEM_LIMIT
        ),
        cost_estimate=pl.CostEstimate(
            flops=2 * 10**9, bytes_accessed=3 * 10**6, transcendentals=10**6
        ),
    )(byte_ids.reshape(1, tokens), queries, key_states, values, cotangent)
    return pl.pallas_call(
        flush,
        out_shape=(out,) * 4,
        in_specs=[pl.BlockSpec(memory_space=pltpu.HBM)] * 4,
        out_specs=(pl.BlockSpec(memory_space=pltpu.HBM),) * 4,
        scratch_shapes=[vmem(queries.shape, BF16)] * 4 + [pltpu.SemaphoreType.DMA((8,))],
        compiler_params=pltpu.CompilerParams(vmem_limit_bytes=VMEM_LIMIT),
    )(*results)


def solution(mesh):
    wide = P("head", None, ("grp", "seq"))
    return jax.shard_map(
        local,
        mesh=mesh,
        in_specs=(P(("grp", "seq")), wide, wide, wide, wide),
        out_specs=(wide,) * 4,
        check_vma=False,
    )
```

```python
import jax
import jax.numpy as jnp
from jax import lax
from jax.experimental import pallas as pl
from jax.experimental.pallas import tpu as pltpu
from jax.sharding import PartitionSpec as P

HEAD = 64
VMEM_LIMIT = 62 * 2**20
BLOCK = 128
SPAN = 256
NEAR_DEAD = -(2.0**96)
FAR_DEAD = -(2.0**90)
F32 = jnp.float32
BF16 = jnp.bfloat16


def nn(a, b):
    return lax.dot_general(a, b, (((1,), (0,)), ((), ())), preferred_element_type=F32)


def nt(a, b):
    return lax.dot_general(a, b, (((1,), (1,)), ((), ())), preferred_element_type=F32)


def tn(a, b):
    return lax.dot_general(a, b, (((0,), (0,)), ((), ())), preferred_element_type=F32)


def split(x):
    high = x.astype(BF16)
    return high, (x - high.astype(F32)).astype(BF16)


def iota(shape, dim):
    return lax.broadcasted_iota(jnp.int32, shape, dim)


def pool_matrix(rows, level):
    shape = (rows, rows << level)
    return jnp.where(iota(shape, 1) // (1 << level) == iota(shape, 0), 1.0, 0.0)


def pool_rows(x, level):
    mat = pool_matrix(x.shape[0] >> level, level).astype(BF16)
    high, low = split(x)
    return nn(mat, high) + nn(mat, low)


def spread_rows(x, level):
    mat = pool_matrix(x.shape[0], level).astype(BF16)
    high, low = split(x)
    return tn(mat, high) + tn(mat, low)


def low_lanes(shape):
    return iota(shape, 1) < HEAD


def key_side(kv, count):
    low = low_lanes(kv.shape)
    mean = pltpu.roll(kv / jnp.maximum(count, 1.0), HEAD, 1)
    mean_only = jnp.where(low, 0.0, mean)
    full = jnp.where(low, jnp.where(count > 0, 0.0, FAR_DEAD), mean)
    return full, mean_only


def value_side(kv, count):
    return jnp.where(low_lanes(kv.shape), count, kv)


def query_side(cq, scale):
    return jnp.where(low_lanes(cq.shape), 1.0, cq * scale)


def product3(a, b):
    ah, al = split(a)
    bh, bl = split(b)
    return nt(
        jnp.concatenate([ah, ah, al], axis=1), jnp.concatenate([bh, bl, bh], axis=1)
    )


def far_forward(query, key_full, value):
    scores = product3(query, key_full)
    top = jnp.max(scores, axis=1, keepdims=True)
    high, low = split(top)
    top = high.astype(F32) + low.astype(F32)
    weights = jnp.exp(scores - top).astype(BF16)
    vh, vl = split(value)
    out = nn(jnp.concatenate([weights, weights], axis=1), jnp.concatenate([vh, vl], axis=0))
    return weights, jnp.where(iota(out.shape, 1) == 0, top, out)


def far_backward(query, key_mean, value, count, weights, row_grad, scale):
    inner = product3(row_grad, value)
    dscore = (weights.astype(F32) * inner).astype(BF16)
    grad_query = nn(dscore, key_mean.astype(BF16)) * scale
    dk = tn(dscore, query.astype(BF16))
    dv = tn(weights, row_grad.astype(BF16))
    dk = pltpu.roll(dk, HEAD, 1) / jnp.maximum(count, 1.0)
    return grad_query, jnp.where(low_lanes(dv.shape), dk, dv)


def kernel(size, refs):
    bits = size.bit_length() - 1
    it = iter(refs)
    sources = [next(it) for _ in range(5)]
    targets = [next(it) for _ in range(4)]
    pall, kv_s, cq_s, wn_s, num_s, top_s, wf_s, fh_s, fl_s, rg_s = (next(it) for _ in range(10))
    gain_s, stat_s, sc_s, dq_s, dkv_s, dv_s = (next(it) for _ in range(6))
    sends = [next(it) for _ in range(bits)]
    recvs = [next(it) for _ in range(bits)]
    back_sends = [next(it) for _ in range(bits)]
    back_recvs = [next(it) for _ in range(bits)]
    send_sem, recv_sem, back_send_sem, back_recv_sem = (next(it) for _ in range(4))
    ids, q_ref, k_ref, v_ref, g_ref = held = [next(it) for _ in range(5)]
    att_ref, gq_ref, gk_ref, gv_ref = results = [next(it) for _ in range(4)]
    in_sem, out_sem = next(it), next(it)
    stores = [pltpu.make_async_copy(x, y, out_sem.at[i]) for i, (x, y) in enumerate(zip(results, targets))]
    loads = [pltpu.make_async_copy(x, y, in_sem.at[i]) for i, (x, y) in enumerate(zip(sources, held))]
    for i in (0, 2, 3, 1, 4):
        loads[i].start()

    tokens = q_ref.shape[2]
    chunks = tokens // SPAN
    local_top = (tokens // BLOCK).bit_length() - 1
    scale = HEAD**-0.5
    me = lax.axis_index("seq")

    def flipped(m):
        out = me
        for bit in range(bits):
            if m >> bit & 1:
                out = out + (1 - 2 * lax.rem(lax.div(me, 1 << bit), 2)) * (1 << bit)
        return out

    barrier = pltpu.get_barrier_semaphore()
    for m in range(1, size):
        pl.semaphore_signal(
            barrier, inc=1, device_id={"seq": flipped(m)}, device_id_type=pl.DeviceIdType.MESH
        )

    start = {}
    at = 0
    for level in range(1, local_top + 1):
        start[level] = at
        at += tokens >> level
    prow = {}
    at = 0
    for level in range(1, local_top + 1):
        prow[level] = at
        at += SPAN >> level
    pooled_rows = at

    pieces = [pool_matrix(SPAN >> level, level) for level in range(1, local_top + 1)]
    pieces.append(jnp.zeros((SPAN - pooled_rows, SPAN), F32))
    pall[...] = jnp.concatenate(pieces, axis=0).astype(BF16)

    def span(p):
        return pl.ds(p * SPAN, SPAN)

    def level_rows(p, level):
        n = SPAN >> level
        return pl.ds(start[level] + p * n, n)

    def pool_slice(level):
        return pl.ds(prow[level], SPAN >> level)

    for i in range(4):
        loads[i].wait()

    for p in range(chunks):
        cols = span(p)
        mask = jnp.where(ids[:, cols] != 0, 1.0, 0.0)
        maskh = jnp.broadcast_to(mask, (HEAD, SPAN))
        km = (k_ref[0, :, cols].astype(F32) * maskh).astype(BF16)
        vm = (v_ref[0, :, cols].astype(F32) * maskh).astype(BF16)
        x = jnp.concatenate([km, vm, maskh.astype(BF16), q_ref[0, :, cols]], axis=0)
        r = nt(pall[...], x)
        for level in range(1, local_top + 1):
            piece = r[prow[level] : prow[level] + (SPAN >> level)]
            kv_s[level_rows(p, level), :] = piece[:, :128]
            cq_s[level_rows(p, level), :] = piece[:, 128:]

    kv = kv_s[pl.ds(start[local_top], BLOCK), :]
    cq = cq_s[pl.ds(start[local_top], BLOCK), :]
    cross_query = []
    for b in range(bits):
        if b:
            kv, cq = pool_rows(kv, 1), pool_rows(cq, 1)
        cross_query.append(query_side(cq, scale * 2.0 ** -(local_top + b)))
        rows = BLOCK >> b
        sends[b][pl.ds(0, rows), :] = kv
        wide = cq if not b else jnp.concatenate([cq, jnp.zeros((BLOCK - rows, 128), F32)], axis=0)
        sends[b][pl.ds(rows, 8), :] = wide.T[:8]

    pl.semaphore_wait(barrier, size - 1)
    copies = []
    for m in reversed(range(1, size)):
        b = m.bit_length() - 1
        copy = pltpu.make_async_remote_copy(
            src_ref=sends[b],
            dst_ref=recvs[b].at[lax.rem(me, 1 << b)],
            send_sem=send_sem.at[m - 1],
            recv_sem=recv_sem.at[m - 1],
            device_id={"seq": flipped(m)},
            device_id_type=pl.DeviceIdType.MESH,
        )
        copy.start()
        copies.append(copy)

    eye = iota((SPAN, SPAN), 0) == iota((SPAN, SPAN), 1)
    first = iota((16, SPAN), 0) == 0
    ones16 = jnp.where(first, 1.0, 0.0).astype(BF16)
    for p in range(chunks):
        cols = span(p)
        q = q_ref[0, :, cols]
        k = k_ref[0, :, cols]
        dead = jnp.where(ids[:, cols] != 0, 0.0, NEAR_DEAD)
        dead = jnp.where(first, dead, 0.0).astype(BF16)
        qf = q.astype(F32) * scale
        own = jnp.sum(qf * k.astype(F32), axis=0, keepdims=True)
        scores = tn(
            jnp.concatenate([k, dead], axis=0), jnp.concatenate([qf.astype(BF16), ones16], axis=0)
        )
        scores = jnp.where(eye, own, scores)
        top = jnp.max(scores, axis=0, keepdims=True)
        w = jnp.exp(scores - top).astype(BF16)
        wn_s[p] = w
        num_s[:, cols] = nn(jnp.concatenate([v_ref[0, :, cols], ones16], axis=0), w)
        top_s[:, cols] = jnp.broadcast_to(top, (8, SPAN))

    def far_operands(level, g):
        own = pl.ds(start[level] + g * BLOCK, BLOCK)
        other = pl.ds(start[level] + (g ^ 1) * BLOCK, BLOCK)
        kv = kv_s[other, :]
        count = cq_s[other, :]
        query = query_side(cq_s[own, :], scale * 2.0**-level)
        return own, other, kv, count, query

    for level in range(1, local_top):
        for g in range((tokens >> level) // BLOCK):
            own, other, kv, count, query = far_operands(level, g)
            w, f = far_forward(query, key_side(kv, count)[0], value_side(kv, count))
            wf_s[own, :] = w
            fh_s[own, :], fl_s[own, :] = split(f)

    cross = []
    for b in range(bits):
        for m in range(1 << b, 2 << b):
            copies[size - 1 - m].wait_recv()
        rows = BLOCK >> b
        parts = [recvs[b][s] for s in range(1 << b)]
        kv = jnp.concatenate([x[:rows] for x in parts], axis=0)
        counts = []
        for x in parts:
            tile = jnp.concatenate([x[rows:]] * (BLOCK // 8), axis=0).T
            counts.append(tile[:rows])
        count = jnp.concatenate(counts, axis=0)
        key_full, key_mean = key_side(kv, count)
        value = value_side(kv, count)
        w, f = far_forward(cross_query[b], key_full, value)
        if b:
            f = spread_rows(f, b)
        cross.append((key_mean, value, count, w, f))
    best = cross[0][4][:, :1]
    for b in range(1, bits):
        best = jnp.maximum(best, cross[b][4][:, :1])
    gains = [jnp.exp(c[4][:, :1] - best) for c in cross]
    total = gains[0] * cross[0][4]
    for b in range(1, bits):
        total = total + gains[b] * cross[b][4]
    total = jnp.where(iota(total.shape, 1) == 0, best, total)
    whole = pl.ds(start[local_top], BLOCK)
    fh_s[whole, :], fl_s[whole, :] = split(total)

    loads[4].wait()

    row64 = iota((HEAD, SPAN), 0)
    for p in range(chunks):
        cols = span(p)
        wide = []
        for level in range(1, local_top + 1):
            rows = level_rows(p, level)
            mat = pall[pool_slice(level), :]
            wide.append(
                tn(
                    jnp.concatenate([fh_s[rows, :], fl_s[rows, :]], axis=0),
                    jnp.concatenate([mat, mat], axis=0),
                )
            )
        near_top = top_s[:1, cols]
        row_top = near_top
        for x in wide:
            row_top = jnp.maximum(row_top, x[:1])
        near_factor = jnp.exp(near_top - row_top)
        near = num_s[:, cols]
        numer = near_factor * near[:HEAD]
        denom = near_factor * near[HEAD : HEAD + 1]
        factors = []
        for x in wide:
            factor = jnp.exp(x[:1] - row_top)
            factors.append(factor)
            numer = numer + factor * x[HEAD:]
            denom = denom + factor * x[1:2]
        inverse = 1.0 / denom
        output = numer * inverse
        att_ref[0, :, cols] = output.astype(BF16)
        g = g_ref[0, :, cols].astype(F32)
        stat = jnp.sum(g * output, axis=0, keepdims=True)
        gain = near_factor * inverse
        gain_s[:, cols] = jnp.broadcast_to(gain, (8, SPAN))
        stat_s[:, cols] = jnp.broadcast_to(stat, (8, SPAN))
        sc_s[:, cols] = (gain * g).astype(BF16)
        for level in range(1, local_top + 1):
            far_gain = factors[level - 1] * inverse
            down = -(far_gain * stat)
            high = down.astype(BF16).astype(F32)
            head = jnp.where(row64 == 0, high, jnp.where(row64 == 1, down - high, 0.0))
            x = jnp.concatenate([head.astype(BF16), (far_gain * g).astype(BF16)], axis=0)
            rg_s[level_rows(p, level), :] = nt(pall[pool_slice(level), :], x)

    stores[0].start()

    base = rg_s[whole, :]
    dq_total = None
    back_copies = []
    for b in reversed(range(bits)):
        key_mean, value, count, w, _ = cross[b]
        row_grad = base * gains[b]
        if b:
            row_grad = pool_rows(row_grad, b)
        dq, dkv = far_backward(
            cross_query[b], key_mean, value, count, w, row_grad, scale * 2.0 ** -(local_top + b)
        )
        rows = BLOCK >> b
        for s in range(1 << b):
            back_sends[b][s] = dkv[s * rows : (s + 1) * rows]
        for m in range(1 << b, 2 << b):
            copy = pltpu.make_async_remote_copy(
                src_ref=back_sends[b].at[lax.rem(flipped(m), 1 << b)],
                dst_ref=back_recvs[b].at[lax.rem(me, 1 << b)],
                send_sem=back_send_sem.at[m - 1],
                recv_sem=back_recv_sem.at[m - 1],
                device_id={"seq": flipped(m)},
                device_id_type=pl.DeviceIdType.MESH,
            )
            copy.start()
            back_copies.append(copy)
        if b:
            dq = spread_rows(dq, b)
        dq_total = dq if dq_total is None else dq_total + dq
    dq_s[whole, :] = dq_total.astype(BF16)

    for level in range(1, local_top):
        for g in range((tokens >> level) // BLOCK):
            own, other, kv, count, query = far_operands(level, g)
            dq, dkv = far_backward(
                query,
                key_side(kv, count)[1],
                value_side(kv, count),
                count,
                wf_s[own, :],
                rg_s[own, :],
                scale * 2.0**-level,
            )
            dq_s[own, :] = dq.astype(BF16)
            dkv_s[other, :] = dkv.astype(BF16)

    for p in range(chunks):
        cols = span(p)
        q, k, v, g = (r[0, :, cols] for r in (q_ref, k_ref, v_ref, g_ref))
        w = wn_s[p]
        dprob = tn(v, g)
        dscore = (
            w.astype(F32) * gain_s[:1, cols] * (dprob - stat_s[:1, cols])
        ).astype(BF16)
        num_s[:HEAD, cols] = nt(q, dscore) * scale
        dv_s[:, cols] = nt(sc_s[:, cols], w)
        gq = nn(k, dscore) * scale
        rows = [level_rows(p, level) for level in range(1, local_top + 1)]
        pad = jnp.zeros((SPAN - pooled_rows, 128), BF16)
        d = jnp.concatenate([dq_s[r, :] for r in rows] + [pad], axis=0)
        gq_ref[0, :, cols] = (gq + tn(d, pall[...])[HEAD:]).astype(BF16)

    stores[1].start()
    for copy in back_copies:
        copy.wait_recv()
    acc = None
    for b in reversed(range(bits)):
        if acc is not None:
            acc = spread_rows(acc, 1)
        for s in range(1 << b):
            acc = back_recvs[b][s] if acc is None else acc + back_recvs[b][s]
    dkv_s[whole, :] = acc.astype(BF16)
    for p in range(chunks):
        cols = span(p)
        rows = [level_rows(p, level) for level in range(1, local_top + 1)]
        pad = jnp.zeros((SPAN - pooled_rows, 128), BF16)
        d = jnp.concatenate([dkv_s[r, :] for r in rows] + [pad], axis=0)
        far = tn(d, pall[...])
        valid = ids[:, cols] != 0
        far = jnp.where(valid, far, 0.0)
        gk_ref[0, :, cols] = (num_s[:HEAD, cols] + far[:HEAD]).astype(BF16)
        gv_ref[0, :, cols] = (dv_s[:, cols] + far[HEAD:]).astype(BF16)
    stores[2].start()
    stores[3].start()
    for copy in copies + back_copies:
        copy.wait_send()
    for store in stores:
        store.wait()


def flush(*refs):
    sem = refs[12]
    loads = [pltpu.make_async_copy(refs[i], refs[8 + i], sem.at[i]) for i in range(4)]
    stores = [pltpu.make_async_copy(refs[8 + i], refs[4 + i], sem.at[4 + i]) for i in range(4)]
    for load in loads:
        load.start()
    for load, store in zip(loads, stores):
        load.wait()
        store.start()
    for store in stores:
        store.wait()


def local(byte_ids, queries, key_states, values, cotangent):
    heads, width, tokens = queries.shape
    size = lax.axis_size("seq")
    bits = size.bit_length() - 1
    chunks = tokens // SPAN
    coarse = tokens - (tokens >> ((tokens // BLOCK).bit_length() - 1))
    vmem = pltpu.VMEM
    scratch = [
        vmem((SPAN, SPAN), BF16),
        vmem((coarse, 128), F32),
        vmem((coarse, 128), F32),
        vmem((chunks, SPAN, SPAN), BF16),
        vmem((HEAD + 16, tokens), F32),
        vmem((8, tokens), F32),
        vmem((coarse, 128), BF16),
        vmem((coarse, 128), BF16),
        vmem((coarse, 128), BF16),
        vmem((coarse, 128), F32),
        vmem((8, tokens), F32),
        vmem((8, tokens), F32),
        vmem((HEAD, tokens), BF16),
        vmem((coarse, 128), BF16),
        vmem((coarse, 128), BF16),
        vmem((HEAD, tokens), F32),
    ]
    scratch += [vmem(((BLOCK >> b) + 8, 128), F32) for b in range(bits)]
    scratch += [vmem((1 << b, (BLOCK >> b) + 8, 128), F32) for b in range(bits)]
    scratch += [vmem((1 << b, BLOCK >> b, 128), F32) for b in range(bits)] * 2
    scratch += [pltpu.SemaphoreType.DMA((size - 1,))] * 4
    scratch += [vmem((1, tokens), jnp.int32)] + [vmem(queries.shape, BF16)] * 8
    scratch += [pltpu.SemaphoreType.DMA((5,)), pltpu.SemaphoreType.DMA((4,))]
    out = jax.ShapeDtypeStruct(queries.shape, BF16)
    results = pl.pallas_call(
        lambda *refs: kernel(size, refs),
        out_shape=(out,) * 4,
        in_specs=[pl.BlockSpec(memory_space=pltpu.HBM)] * 5,
        out_specs=(pl.BlockSpec(memory_space=pltpu.HBM),) * 4,
        scratch_shapes=scratch,
        compiler_params=pltpu.CompilerParams(
            collective_id=0, has_side_effects=True, vmem_limit_bytes=VMEM_LIMIT
        ),
        cost_estimate=pl.CostEstimate(
            flops=2 * 10**9, bytes_accessed=3 * 10**6, transcendentals=10**6
        ),
    )(byte_ids.reshape(1, tokens), queries, key_states, values, cotangent)
    return pl.pallas_call(
        flush,
        out_shape=(out,) * 4,
        in_specs=[pl.BlockSpec(memory_space=pltpu.HBM)] * 4,
        out_specs=(pl.BlockSpec(memory_space=pltpu.HBM),) * 4,
        scratch_shapes=[vmem(queries.shape, BF16)] * 4 + [pltpu.SemaphoreType.DMA((8,))],
        compiler_params=pltpu.CompilerParams(vmem_limit_bytes=VMEM_LIMIT),
    )(*results)


def solution(mesh):
    wide = P("head", None, ("grp", "seq"))
    return jax.shard_map(
        local,
        mesh=mesh,
        in_specs=(P(("grp", "seq")), wide, wide, wide, wide),
        out_specs=(wide,) * 4,
        check_vma=False,
    )
```
